32 devices in a mesh: groups: 2 (over x), tensor: 16 (over z, y, core).
Axes of the slice: x: 2, y: 2, z: 4, core: 2. Of those that a mesh axis runs over, the one named last changes fastest.
Arguments:
- check_hidden_input: bfloat16 [2048, 8192], P('groups', 'tensor'), parts along dimension 0, may hold values from -6 to 6
- query_base_matrix: bfloat16 [16384, 8192], P(('groups', 'tensor')), parts along dimension 0, may hold values from -2 to 2
- adapter_input_factor: bfloat16 [16384, 32], P(('groups', 'tensor')), parts along dimension 0, may hold values from -0.1796875 to 0.1796875
- adapter_output_factor: bfloat16 [64, 8192], P('groups'), parts along dimension 0, may hold values from -1 to 1
- magnitude: float32 [16384], P('groups'), parts along dimension 0, may hold values from 0.5 to 4
- token_document_index: int32 [2048], P('groups'), parts along dimension 0, may hold values from 0 to 3, never falling along the last dimension, each value on 1 to 512 neighbouring positions
- keys: bfloat16 [2048, 1024], P('groups'), parts along dimension 0, may hold values from -300 to 300
- values: bfloat16 [2048, 1024], P('groups'), parts along dimension 0, may hold values from -6 to 6
Outputs:
- merged_weight: float32 [16384, 8192], P('groups', 'tensor'), parts along dimension 0
- attended: bfloat16 [2048, 8192], P('groups', 'tensor'), parts along dimension 0
The draws below stay inside these ranges and needn't reach their ends.
There are 2 independent parts, one for each index of `groups`. The reference program is written for one: setup_inputs(seed, part) draws one part's arguments, and reference() takes and returns one part's arrays. A program takes and returns all parts, laid end to end along the dimension named above; each array names one. Nothing has to cross between parts.
Inputs may be any that keep to these rules, and one draw needn't show every extreme that they name: `token_document_index`: never falling; each document holds 1 to 512 tokens, one exactly 512.
All inputs are finite; a program needn't handle non-finite values.
Results may differ from the reference program's by a relative error of at most 0.0058.
Values may be sent and summed in bfloat16 or wider, within the bound.
No kernel may reach another device: no remote copies, remote signals or barrier semaphores. Data moves between devices by JAX's collectives and lax.ppermute only.
A program may use at most 128 MiB of HBM per device.

```python
import math
import jax
import jax.numpy as jnp
import numpy as np
from jax import lax

MODEL_WIDTH = 8192
H = 64
HD = 128
KVH = 8
UPDATE_RANK = 32
TOK = 1024
QUERY_FEATURES = 8192
KVD = 1024
GROUP = 8


def draw_query_base_matrix(key, part):
    key = jax.random.fold_in(key, 11)
    key_rows, key_cols, key_vals = jax.random.split(key, 3)
    row_scale = jnp.exp(jax.random.uniform(key_rows, (MODEL_WIDTH, 1), jnp.float32) * jnp.log(10.0))
    col_scale = jnp.exp(jax.random.uniform(key_cols, (1, QUERY_FEATURES), jnp.float32) * jnp.log(10.0))
    entries = jax.random.normal(key_vals, (MODEL_WIDTH, QUERY_FEATURES), jnp.float32)
    entries = jnp.clip(entries, -4.0, 4.0) * (0.05 * MODEL_WIDTH ** (-0.5))
    return (entries * row_scale * col_scale).astype(jnp.bfloat16)


def draw_keys(key, part):
    key = jax.random.fold_in(key, 23)
    key_vals = jax.random.fold_in(key, 0)
    entries = jnp.clip(jax.random.normal(key_vals, (TOK, KVD), jnp.float32), -6.0, 6.0)
    return entries.astype(jnp.bfloat16)


def steps_of(own_key, dims, cuts, low, high):
    factor_of, own = 1.0, jax.random.fold_in(own_key, 6)
    for dim, parts in cuts:
        heights = jnp.exp(jax.random.uniform(jax.random.fold_in(own, dim), (parts,), jnp.float32, low / len(cuts), high / len(cuts)))
        factor_of = factor_of * jnp.repeat(heights, dims[dim] // parts).reshape([-1 if axis == dim else 1 for axis in range(len(dims))])
    return factor_of


def split_up(number_of, total, bound, skew):
    portions = [(1 << 20) // math.isqrt(grade ** skew) + 1 for grade in range(2, number_of + 1)]
    rest, given = total - bound - (number_of - 1), [1] * (number_of - 1)
    while rest > 0:
        free = [i for i in range(number_of - 1) if given[i] < bound]
        mass, remaining = sum([portions[i] for i in free]), rest
        for i in free:
            more = min(bound - given[i], max(1, remaining * portions[i] // mass), rest)
            given[i] = given[i] + more
            rest = rest - more
    return np.array([bound] + given)


def uneven(own_key, number_of, total, bound, skew):
    if number_of == 2:
        one = jax.random.randint(own_key, (), max(1, total - bound), min(bound, total - 1) + 1)
        return jnp.stack([one, total - one])
    lengths = jnp.asarray(split_up(number_of, total, bound, skew), jnp.int32)
    couples = (number_of - 1) // 2
    giver, taker = lengths[1:1 + 2 * couples:2], lengths[2:2 + 2 * couples:2]
    room = jnp.minimum(giver - 1, bound - taker)
    passed = jax.random.randint(jax.random.fold_in(own_key, 1), (couples,), 0, 1 << 20) % (room + 1)
    lengths = lengths.at[1:1 + 2 * couples:2].set(giver - passed).at[2:2 + 2 * couples:2].set(taker + passed)
    return lengths[jax.random.permutation(jax.random.fold_in(own_key, 2), number_of)]


def noise(own_key, extent, width, bound, pieces=(), kind=jnp.bfloat16):
    factor_of = steps_of(own_key, extent, pieces, -0.22, 0.18) if pieces else 1.0
    drawn = jax.random.normal(own_key, extent, jnp.float32) * width * factor_of
    return jnp.minimum(jnp.maximum(drawn, -bound), bound).astype(kind)


def setup_inputs(seed: int = 0, part: int = 0) -> dict:
    key_of = jax.random.split(jax.random.key(seed), 9)
    part_splits = jax.random.split(jax.random.fold_in(key_of[8], part), 9)
    check_hidden_input = noise(part_splits[0], (TOK, MODEL_WIDTH), 1.0, 6.0, ((1, 16),))
    query_base_matrix = draw_query_base_matrix(jax.random.fold_in(jax.random.fold_in(key_of[8], part), 71), part)
    adapter_input_factor = noise(part_splits[2], (MODEL_WIDTH, UPDATE_RANK), 0.03, 0.1796875, ((0, 16),))
    adapter_output_factor = noise(part_splits[3], (UPDATE_RANK, QUERY_FEATURES), UPDATE_RANK ** -0.5, 1.0)
    magnitude = jnp.clip(jnp.exp(jax.random.uniform(part_splits[4], (QUERY_FEATURES,), jnp.float32, math.log(0.5), math.log(4.0))), 0.5, 4.0)
    token_document_index = jnp.searchsorted(jnp.cumsum(uneven(part_splits[5], 4, TOK, TOK // 2, 1)), jnp.arange(TOK), side="right").astype(jnp.int32)
    keys = draw_keys(jax.random.fold_in(jax.random.fold_in(key_of[8], part), 71), part)
    values = noise(part_splits[7], (TOK, KVD), 1.0, 6.0)
    return dict(check_hidden_input=check_hidden_input, query_base_matrix=query_base_matrix, adapter_input_factor=adapter_input_factor, adapter_output_factor=adapter_output_factor, magnitude=magnitude, token_document_index=token_document_index, keys=keys, values=values)


def doc_positions(token_document_index):
    count = token_document_index.shape[0]
    index = jnp.arange(count, dtype=jnp.int32)
    starts = jnp.concatenate([jnp.ones((1,), dtype=bool), token_document_index[1:] != token_document_index[:-1]])
    first = lax.cummax(jnp.where(starts, index, jnp.int32(0)), axis=0)
    return (index - first).astype(jnp.float32)

def rotate(query, position):
    half = query.shape[-1] // 2
    freqs = 500000.0 ** (-(jnp.arange(half, dtype=jnp.float32) * 2.0 / query.shape[-1]))
    angle = position[:, None] * freqs[None, :]
    cosine = jnp.cos(angle)[:, None, :]
    sine = jnp.sin(angle)[:, None, :]
    first_half = query[..., :half]
    second_half = query[..., half:]
    return jnp.concatenate([first_half * cosine - second_half * sine, second_half * cosine + first_half * sine], axis=-1)

def attend_head(query_head, key_head, value_head, allowed):
    scores = jnp.dot(query_head, key_head.T, preferred_element_type=jnp.float32) / jnp.sqrt(jnp.float32(query_head.shape[-1]))
    scores = jnp.where(allowed, scores, -jnp.inf)
    top = lax.optimization_barrier(jnp.max(scores, axis=1, keepdims=True))
    weights = jnp.exp(scores - top)
    probs = (weights / lax.optimization_barrier(jnp.sum(weights, axis=1, keepdims=True))).astype(jnp.bfloat16)
    return jnp.dot(probs, value_head, preferred_element_type=jnp.float32).astype(jnp.bfloat16)

def reference(check_hidden_input, query_base_matrix, adapter_input_factor, adapter_output_factor, magnitude, token_document_index, keys, values):
    updated_weight = query_base_matrix.astype(jnp.float32) + jnp.dot(adapter_input_factor, adapter_output_factor, preferred_element_type=jnp.float32)
    col_norm_sq = lax.optimization_barrier(jnp.sum(updated_weight * updated_weight, axis=0))
    merged_weight = updated_weight * (magnitude / jnp.sqrt(col_norm_sq + 1e-06))[None, :]
    serve_weight = merged_weight.astype(jnp.bfloat16)
    query = jnp.dot(check_hidden_input, serve_weight, preferred_element_type=jnp.float32)
    tokens = query.shape[0]
    position = doc_positions(token_document_index)
    rotated = rotate(query.reshape(tokens, H, HD), position).astype(jnp.bfloat16)
    index = jnp.arange(tokens, dtype=jnp.int32)
    allowed = (index[None, :] <= index[:, None]) & (token_document_index[None, :] == token_document_index[:, None])
    key_heads = keys.reshape(tokens, KVH, HD)
    value_heads = values.reshape(tokens, KVH, HD)

    def one_head(head):
        kv_head = head // GROUP
        query_head = lax.dynamic_index_in_dim(rotated, head, axis=1, keepdims=False)
        key_head = lax.dynamic_index_in_dim(key_heads, kv_head, axis=1, keepdims=False)
        value_head = lax.dynamic_index_in_dim(value_heads, kv_head, axis=1, keepdims=False)
        return attend_head(query_head, key_head, value_head, allowed)
    outputs = lax.map(one_head, jnp.arange(H, dtype=jnp.int32))
    attended = jnp.transpose(outputs, (1, 0, 2)).reshape(tokens, H * HD)
    return (merged_weight, attended)
```

```python
import functools

import jax
import jax.numpy as jnp
from jax import lax
from jax.experimental import pallas as pl
from jax.experimental.pallas import tpu as pltpu
from jax.sharding import PartitionSpec as P

HD = 128
KVH = 8
GROUP = 8
DOC_MAX = 512
Q_BLOCK = 256


def doc_positions(token_document_index):
    count = token_document_index.shape[0]
    index = jnp.arange(count, dtype=jnp.int32)
    starts = jnp.concatenate(
        [jnp.ones((1,), dtype=bool), token_document_index[1:] != token_document_index[:-1]]
    )
    first = lax.cummax(jnp.where(starts, index, jnp.int32(0)), axis=0)
    return (index - first).astype(jnp.float32)


def rope_tables(position):
    half = HD // 2
    freqs = 500000.0 ** (-(jnp.arange(half, dtype=jnp.float32) * 2.0 / HD))
    angle = position[:, None] * freqs[None, :]
    cosine = jnp.cos(angle)
    sine = jnp.sin(angle)
    return jnp.concatenate([cosine, cosine], axis=1), jnp.concatenate([-sine, sine], axis=1)


def cut_kernel(me_ref, a_ref, b_ref, w_ref, *refs):
    outs, sums_ref, (stage, in_sem, out_sem) = refs[:-4], refs[-4], refs[-3:]
    me = me_ref[0]
    n, _, width = stage.shape

    def column(e):
        return pl.multiple_of((me ^ e) * width, width)

    order = (8, 12, 9, 13, 4, 10, 14, 5, 11, 15, 6, 7, 2, 3, 1, 0)
    reads = {
        e: pltpu.make_async_copy(w_ref.at[:, pl.ds(column(e), width)], stage.at[e], in_sem.at[e])
        for e in order
    }
    writes = {e: pltpu.make_async_copy(stage.at[e], outs[e], out_sem.at[e]) for e in order}
    for e in order:
        reads[e].start()
    for e in order:
        reads[e].wait()
        writes[e].start()
        updated = stage[e].astype(jnp.float32) + jnp.dot(
            a_ref[...], b_ref[:, pl.ds(column(e), width)], preferred_element_type=jnp.float32
        )
        part = jnp.sum((updated * updated).reshape(-1, 8, width), axis=0)
        sums_ref[pl.ds(e, 1), :] = jnp.sum(part, axis=0, keepdims=True)
    for e in order:
        writes[e].wait()


def cut(me, a, b, w):
    rows, width = w.shape[0], w.shape[1] // 16
    vmem, hbm = pl.BlockSpec(memory_space=pltpu.VMEM), pl.BlockSpec(memory_space=pl.ANY)
    *blocks, sums = pl.pallas_call(
        cut_kernel,
        out_shape=[jax.ShapeDtypeStruct((rows, width), w.dtype)] * 16
        + [jax.ShapeDtypeStruct((16, width), jnp.float32)],
        in_specs=[pl.BlockSpec(memory_space=pltpu.SMEM), vmem, vmem, hbm],
        out_specs=[hbm] * 16 + [vmem],
        scratch_shapes=[
            pltpu.VMEM((16, rows, width), w.dtype),
            pltpu.SemaphoreType.DMA((16,)),
            pltpu.SemaphoreType.DMA((16,)),
        ],
        compiler_params=pltpu.CompilerParams(vmem_limit_bytes=24 * 1024 * 1024),
        cost_estimate=pl.CostEstimate(
            flops=4 * w.size, bytes_accessed=4 * w.size, transcendentals=0
        ),
    )(me, a, b, w)
    return blocks, sums


def merge_kernel(plan, me_ref, b_ref, mag_ref, total_ref, *refs):
    (slots, xor, rows, w_at, x_at, n_w, n_x, local, first, last) = plan
    w_refs, refs = refs[:n_w], refs[n_w:]
    x_refs, refs = refs[:n_x], refs[n_x:]
    if last:
        (cos_ref, sin_ref, row_ref, col_ref, k_ref, v_ref), refs = refs[:6], refs[6:]
    if not first:
        (q_in, _), refs = refs[:2], refs[2:]
    (merged_ref, q_out), refs = refs[:2], refs[2:]
    (w_buf, x_buf, a_buf, u_buf, w_sem, x_sem, a_sem, m_sem), refs = refs[:8], refs[8:]
    if last:
        q_buf, k_buf, v_buf, k_sem, q_sem, o_sem = refs
    else:
        q_buf = q_out
    tokens = x_buf.shape[1]
    me = me_ref[0]
    count = len(slots)

    def part(refs, spot):
        which, index = spot
        return refs[which] if index is None else refs[which].at[index]

    def w_copy(k):
        return pltpu.make_async_copy(part(w_refs, w_at[k]), w_buf.at[k], w_sem.at[k])

    def x_copy(k):
        src = part(x_refs, x_at[k]).at[pl.ds(0, tokens)]
        return pltpu.make_async_copy(src, x_buf.at[k], x_sem.at[k])

    def a_copy(k):
        src = part(x_refs, x_at[k]).at[pl.ds(tokens, a_buf.shape[1])]
        return pltpu.make_async_copy(src, a_buf.at[k], a_sem.at[k])

    def out_copy(k):
        row = pl.multiple_of(((me ^ slots[k]) if xor else slots[k]) * rows, rows)
        return pltpu.make_async_copy(u_buf.at[k], merged_ref.at[pl.ds(row, rows), :], m_sem.at[k])

    for k in range(count):
        w_copy(k).start()
        a_copy(k).start()
        x_copy(k).start()
    if last:
        column = pl.multiple_of(me * local // GROUP * HD, HD)
        kv_copies = [
            pltpu.make_async_copy(ref.at[:, pl.ds(column, HD)], buf, k_sem.at[j])
            for j, (ref, buf) in enumerate(((k_ref, k_buf), (v_ref, v_buf)))
        ]
        for copy in kv_copies:
            copy.start()
        if not first:
            q_copy = pltpu.make_async_copy(q_in, q_buf, q_sem)
            q_copy.start()

    scale = mag_ref[...] / jnp.sqrt(total_ref[...] + 1e-06)
    for k in range(count):
        w_copy(k).wait()
        a_copy(k).wait()
        updated = w_buf[k].astype(jnp.float32) + lax.dot_general(
            a_buf[k], b_ref[...], (((0,), (0,)), ((), ())), preferred_element_type=jnp.float32
        )
        merged = updated * scale
        u_buf[k] = merged
        out_copy(k).start()
        x_copy(k).wait()
        product = jnp.dot(x_buf[k], merged.astype(jnp.bfloat16), preferred_element_type=jnp.float32)
        if k == 0 and first:
            q_buf[...] = product
        elif k == 0 and not last:
            q_buf[...] = q_in[...] + product
        else:
            if k == 0:
                q_copy.wait()
            q_buf[...] += product

    if last:
        for copy in kv_copies:
            copy.wait()
        attend(q_buf, cos_ref, sin_ref, row_ref, col_ref, k_buf, v_buf, q_out, local)
    for k in range(count):
        out_copy(k).wait()


def attend(q_ref, cos_ref, sin_ref, row_ref, col_ref, k_ref, v_ref, att_ref, local):
    tokens = q_ref.shape[0]
    for t in range(0, tokens, Q_BLOCK):
        low, high = max(0, t - DOC_MAX), t + Q_BLOCK
        shape = (Q_BLOCK, high - low)
        later = lax.broadcasted_iota(jnp.int32, shape, 0) + (t - low)
        allowed = (lax.broadcasted_iota(jnp.int32, shape, 1) <= later) & (
            row_ref[:, pl.ds(low, high - low)] == col_ref[pl.ds(t, Q_BLOCK), :]
        )
        cosine, sine = cos_ref[pl.ds(t, Q_BLOCK), :], sin_ref[pl.ds(t, Q_BLOCK), :]
        for h in range(local):
            lanes = pl.ds(h * HD, HD)
            query = q_ref[pl.ds(t, Q_BLOCK), lanes]
            turned = pltpu.roll(query, HD // 2, 1)
            rotated = (query * cosine + turned * sine).astype(jnp.bfloat16)
            scores = lax.dot_general(
                rotated,
                k_ref[pl.ds(low, high - low), :],
                (((1,), (1,)), ((), ())),
                preferred_element_type=jnp.float32,
            ) * jnp.float32(HD**-0.5)
            scores = jnp.where(allowed, scores, -jnp.inf)
            top = jnp.max(scores, axis=1, keepdims=True)
            weights = jnp.exp(scores - top)
            probs = (weights / jnp.sum(weights, axis=1, keepdims=True)).astype(jnp.bfloat16)
            att_ref[pl.ds(t, Q_BLOCK), lanes] = jnp.dot(
                probs, v_ref[pl.ds(low, high - low), :], preferred_element_type=jnp.float32
            ).astype(jnp.bfloat16)


def merge(me, b, mag, total, slots, w_list, w_at, x_list, x_at, sizes, xor, previous=None, attention=None):
    features, rows, tokens, rank = sizes
    width, count = b.shape[1], len(slots)
    first, last = previous is None, attention is not None
    plan = (slots, xor, rows, w_at, x_at, len(w_list), len(x_list), width // HD, first, last)
    vmem, hbm = pl.BlockSpec(memory_space=pltpu.VMEM), pl.BlockSpec(memory_space=pl.ANY)
    operands = [me, b, mag, total, *w_list, *x_list]
    in_specs = [pl.BlockSpec(memory_space=pltpu.SMEM)] + [vmem] * 3 + [hbm] * (len(w_list) + len(x_list))
    scratch = [
        pltpu.VMEM((count, rows, width), jnp.bfloat16),
        pltpu.VMEM((count, tokens, rows), jnp.bfloat16),
        pltpu.VMEM((count, rank, rows), jnp.bfloat16),
        pltpu.VMEM((count, rows, width), jnp.float32),
    ] + [pltpu.SemaphoreType.DMA((count,))] * 4
    if last:
        operands += list(attention)
        in_specs += [vmem] * 4 + [hbm] * 2
        scratch += [
            pltpu.VMEM((tokens, width), jnp.float32),
            pltpu.VMEM((tokens, HD), jnp.bfloat16),
            pltpu.VMEM((tokens, HD), jnp.bfloat16),
            pltpu.SemaphoreType.DMA((2,)),
            pltpu.SemaphoreType.DMA,
            pltpu.SemaphoreType.DMA,
        ]
    aliases = {}
    if not first:
        merged, query = previous
        operands += [query, merged]
        in_specs += [hbm if last else vmem, hbm]
        aliases = {len(operands) - 1: 0}
    return pl.pallas_call(
        functools.partial(merge_kernel, plan),
        out_shape=[
            jax.ShapeDtypeStruct((features, width), jnp.float32),
            jax.ShapeDtypeStruct((tokens, width), jnp.bfloat16 if last else jnp.float32),
        ],
        in_specs=in_specs,
        out_specs=[hbm, vmem],
        scratch_shapes=scratch,
        input_output_aliases=aliases,
        compiler_params=pltpu.CompilerParams(vmem_limit_bytes=48 * 1024 * 1024),
        cost_estimate=pl.CostEstimate(
            flops=2 * tokens * count * rows * width,
            bytes_accessed=count * rows * (6 * width + 2 * tokens),
            transcendentals=width // HD * tokens * tokens if last else 0,
        ),
    )(*operands)


def after(array, others):
    if not others:
        return array
    return lax.optimization_barrier((array, *others))[0]


ROUNDS = (
    ("z2", "z1", "y0", "s1", "w2", "s2", "s4"),
    ("z3", "y1", "y2", "w8", "w12"),
    ("y3", "cA", "w9", "w13", "w4"),
    ("cD", "w10", "w14", "w5", "w3", "s8"),
    ("w11", "w15", "w6", "w7", "w1"),
)
LINES = {"z1": ("x", 4), "z2": ("x", 8), "z3": ("z2", 4), "y0": ("x", 2), "y1": ("z1", 2), "y2": ("z2", 2), "y3": ("z3", 2)}
STACKS = {"cA": ("x", "z1", "z2", "y0"), "cD": ("z3", "y1", "y2", "y3")}
GROUPS = ((0, 8, 12, 4, 9, 2), (13, 10, 14, 5, 3), (6, 7, 1), (11, 15))


def exchange(x, blocks, sums):
    def swap(array, d):
        return lax.ppermute(array, "tensor", [(i, i ^ d) for i in range(16)])

    got = {"x": x}
    partial = sums.reshape(8, 2, -1)

    def payload(name):
        if name in LINES:
            return got[LINES[name][0]], LINES[name][1]
        if name in STACKS:
            return jnp.stack([got[k] for k in STACKS[name]]), 1
        d = int(name[1:])
        return (partial[:, 1] if name[0] == "s" else blocks[d]), d

    def heavy(name):
        return name[0] == "w"

    for k, names in enumerate(ROUNDS):
        new = {}
        for name in names:
            gates = [m for m in ROUNDS[k - 1] if not (heavy(name) and heavy(m))] if k else []
            gates += ROUNDS[k - 2] if k > 1 else ()
            array, d = payload(name)
            new[name] = swap(after(array, [got[m] for m in gates]), d)
            if name[0] == "s":
                partial = partial[:, 0] + new[name]
                if d < 8:
                    partial = partial.reshape(4 // d, 2, -1)
        got.update(new)
    x_list = [got[k] for k in ("x", "z1", "z2", "z3", "y0", "y1", "y2", "y3", "cA", "cD")]
    x_at = [None] * 16
    for k, d in enumerate((0, 4, 8, 12, 2, 6, 10, 14)):
        x_at[d] = (k, None)
    for k, d in enumerate((1, 5, 9, 3)):
        x_at[d] = (8, k)
    for k, d in enumerate((13, 7, 11, 15)):
        x_at[d] = (9, k)
    weights = [blocks[0]] + [got["w" + str(d)] for d in range(1, 16)]
    return x_list, x_at, weights, partial


def shards(
    check_hidden_input,
    query_base_matrix,
    adapter_input_factor,
    adapter_output_factor,
    magnitude,
    token_document_index,
    keys,
    values,
):
    n = lax.axis_size("tensor")
    my_index = lax.axis_index("tensor")
    rows, features = query_base_matrix.shape
    tokens, rank = check_hidden_input.shape[0], adapter_output_factor.shape[0]
    width = features // n
    me = my_index.astype(jnp.int32).reshape(1)
    b = lax.dynamic_slice_in_dim(adapter_output_factor, my_index * width, width, axis=1)
    mag = lax.dynamic_slice_in_dim(magnitude, my_index * width, width, axis=0)[None, :]
    cosine, sine = rope_tables(doc_positions(token_document_index))
    x = jnp.concatenate([check_hidden_input, adapter_input_factor.T], axis=0)
    attention = (cosine, sine, token_document_index[None, :], token_document_index[:, None], keys, values)
    sizes = (n * rows, rows, tokens, rank)
    if n == 16:
        blocks, sums = cut(me, adapter_input_factor, adapter_output_factor, query_base_matrix)
        x_list, x_at, weights, total = exchange(x, blocks, sums)
        done = None
        for k, slots in enumerate(GROUPS):
            used = sorted({x_at[d][0] for d in slots})
            done = merge(
                me, b, mag, total, slots,
                [weights[d] for d in slots], [(j, None) for j in range(len(slots))],
                [x_list[j] for j in used], [(used.index(x_at[d][0]), x_at[d][1]) for d in slots],
                sizes, True, done, attention if k == len(GROUPS) - 1 else None,
            )
        return done[0], done[1]
    x_all = lax.all_gather(x, "tensor", axis=0)
    w_cut = jnp.transpose(query_base_matrix.reshape(rows, n, width), (1, 0, 2))
    w_all = lax.all_to_all(w_cut, "tensor", split_axis=0, concat_axis=0, tiled=True)
    low_rank = lax.dot_general(x_all[:, tokens:], b, (((1,), (0,)), ((), ())), preferred_element_type=jnp.float32)
    total = jnp.sum(jnp.square(w_all.astype(jnp.float32) + low_rank), axis=(0, 1))[None, :]
    slots = tuple(range(n))
    at = [(0, d) for d in slots]
    merged, attended = merge(me, b, mag, total, slots, [w_all], at, [x_all], at, sizes, False, None, attention)
    return merged, attended


def solution(mesh):
    placed = (
        P("groups", "tensor"),
        P(("groups", "tensor"), None),
        P(("groups", "tensor"), None),
        P("groups", None),
        P("groups"),
        P("groups"),
        P("groups", None),
        P("groups", None),
    )
    return jax.shard_map(
        shards,
        mesh=mesh,
        in_specs=placed,
        out_specs=(P("groups", "tensor"), P("groups", "tensor")),
        check_vma=False,
    )
```

```python
import functools
import math

import jax
import jax.numpy as jnp
from jax import lax
from jax.experimental import pallas as pl
from jax.experimental.pallas import tpu as pltpu
from jax.sharding import PartitionSpec as P

HD = 128
KVH = 8
GROUP = 8
DOC_MAX = 512
Q_BLOCK = 128


def doc_positions(token_document_index):
    count = token_document_index.shape[0]
    index = jnp.arange(count, dtype=jnp.int32)
    starts = jnp.concatenate(
        [jnp.ones((1,), dtype=bool), token_document_index[1:] != token_document_index[:-1]]
    )
    first = lax.cummax(jnp.where(starts, index, jnp.int32(0)), axis=0)
    return (index - first).astype(jnp.float32)


def rope_tables(position):
    half = HD // 2
    freqs = 500000.0 ** (-(jnp.arange(half, dtype=jnp.float32) * 2.0 / HD))
    angle = position[:, None] * freqs[None, :]
    cosine = jnp.cos(angle)
    sine = jnp.sin(angle)
    return jnp.concatenate([cosine, cosine], axis=1), jnp.concatenate([-sine, sine], axis=1)


def cut_kernel(me_ref, a_ref, b_ref, w_ref, *refs):
    outs, sums_ref, (stage, in_sem, out_sem) = refs[:-4], refs[-4], refs[-3:]
    me = me_ref[0]
    n, _, width = stage.shape

    def column(e):
        return pl.multiple_of((me ^ e) * width, width)

    order = (8, 12, 9, 13, 4, 10, 14, 5, 11, 15, 6, 7, 2, 3, 1, 0)
    reads = {
        e: pltpu.make_async_copy(w_ref.at[:, pl.ds(column(e), width)], stage.at[e], in_sem.at[e])
        for e in order
    }
    writes = {e: pltpu.make_async_copy(stage.at[e], outs[e], out_sem.at[e]) for e in order}
    for e in order:
        reads[e].start()
    for e in order:
        reads[e].wait()
        writes[e].start()
        updated = stage[e].astype(jnp.float32) + jnp.dot(
            a_ref[...], b_ref[:, pl.ds(column(e), width)], preferred_element_type=jnp.float32
        )
        part = jnp.sum((updated * updated).reshape(-1, 8, width), axis=0)
        sums_ref[pl.ds(e, 1), :] = jnp.sum(part, axis=0, keepdims=True)
    for e in order:
        writes[e].wait()


def cut(me, a, b, w):
    rows, width = w.shape[0], w.shape[1] // 16
    vmem, hbm = pl.BlockSpec(memory_space=pltpu.VMEM), pl.BlockSpec(memory_space=pl.ANY)
    *blocks, sums = pl.pallas_call(
        cut_kernel,
        out_shape=[jax.ShapeDtypeStruct((rows, width), w.dtype)] * 16
        + [jax.ShapeDtypeStruct((16, width), jnp.float32)],
        in_specs=[pl.BlockSpec(memory_space=pltpu.SMEM), vmem, vmem, hbm],
        out_specs=[hbm] * 16 + [vmem],
        scratch_shapes=[
            pltpu.VMEM((16, rows, width), w.dtype),
            pltpu.SemaphoreType.DMA((16,)),
            pltpu.SemaphoreType.DMA((16,)),
        ],
        compiler_params=pltpu.CompilerParams(vmem_limit_bytes=24 * 1024 * 1024),
        cost_estimate=pl.CostEstimate(
            flops=4 * w.size, bytes_accessed=4 * w.size, transcendentals=0
        ),
    )(me, a, b, w)
    return blocks, sums


def merge_kernel(plan, me_ref, b_ref, mag_ref, total_ref, *refs):
    (slots, xor, rows, w_at, x_at, n_w, n_x, local, first, last) = plan
    w_refs, refs = refs[:n_w], refs[n_w:]
    x_refs, refs = refs[:n_x], refs[n_x:]
    if last:
        (cos_ref, sin_ref, row_ref, col_ref, k_ref, v_ref), refs = refs[:6], refs[6:]
    if not first:
        (q_in, _), refs = refs[:2], refs[2:]
    (merged_ref, q_out), refs = refs[:2], refs[2:]
    (w_buf, x_buf, a_buf, u_buf, w_sem, x_sem, a_sem, m_sem), refs = refs[:8], refs[8:]
    if last:
        q_buf, k_buf, v_buf, k_sem = refs
    else:
        q_buf = q_out
    tokens = x_buf.shape[1]
    me = me_ref[0]
    count = len(slots)

    def part(refs, spot):
        which, index = spot
        return refs[which] if index is None else refs[which].at[index]

    def w_copy(k):
        return pltpu.make_async_copy(part(w_refs, w_at[k]), w_buf.at[k], w_sem.at[k])

    def x_copy(k):
        src = part(x_refs, x_at[k]).at[pl.ds(0, tokens)]
        return pltpu.make_async_copy(src, x_buf.at[k], x_sem.at[k])

    def a_copy(k):
        src = part(x_refs, x_at[k]).at[pl.ds(tokens, a_buf.shape[1])]
        return pltpu.make_async_copy(src, a_buf.at[k], a_sem.at[k])

    def out_copy(k):
        row = pl.multiple_of(((me ^ slots[k]) if xor else slots[k]) * rows, rows)
        return pltpu.make_async_copy(u_buf.at[k], merged_ref.at[pl.ds(row, rows), :], m_sem.at[k])

    for k in range(count):
        w_copy(k).start()
        a_copy(k).start()
        x_copy(k).start()
    if last:
        column = pl.multiple_of(me * local // GROUP * HD, HD)
        kv_copies = [
            pltpu.make_async_copy(ref.at[:, pl.ds(column, HD)], buf, k_sem.at[j])
            for j, (ref, buf) in enumerate(((k_ref, k_buf), (v_ref, v_buf)))
        ]
        for copy in kv_copies:
            copy.start()

    scale = mag_ref[...] / jnp.sqrt(total_ref[...] + 1e-06)
    for k in range(count):
        w_copy(k).wait()
        a_copy(k).wait()
        updated = w_buf[k].astype(jnp.float32) + lax.dot_general(
            a_buf[k], b_ref[...], (((0,), (0,)), ((), ())), preferred_element_type=jnp.float32
        )
        merged = updated * scale
        u_buf[k] = merged
        out_copy(k).start()
        x_copy(k).wait()
        product = jnp.dot(x_buf[k], merged.astype(jnp.bfloat16), preferred_element_type=jnp.float32)
        if k > 0:
            q_buf[...] += product
        elif first:
            q_buf[...] = product
        else:
            q_buf[...] = q_in[...] + product

    if last:
        for copy in kv_copies:
            copy.wait()
        attend(q_buf, cos_ref, sin_ref, row_ref, col_ref, k_buf, v_buf, q_out, local)
    for k in range(count):
        out_copy(k).wait()


def attend(q_ref, cos_ref, sin_ref, row_ref, col_ref, k_ref, v_ref, att_ref, local):
    tokens = q_ref.shape[0]
    turns = jnp.float32(HD**-0.5 * math.log2(math.e))
    for t in range(0, tokens, Q_BLOCK):
        low, high = max(0, t - DOC_MAX), t + Q_BLOCK
        shape = (Q_BLOCK, high - low)
        later = lax.broadcasted_iota(jnp.int32, shape, 0) + (t - low)
        allowed = (lax.broadcasted_iota(jnp.int32, shape, 1) <= later) & (
            row_ref[:, pl.ds(low, high - low)] == col_ref[pl.ds(t, Q_BLOCK), :]
        )
        cosine, sine = cos_ref[pl.ds(t, Q_BLOCK), :], sin_ref[pl.ds(t, Q_BLOCK), :]
        rotated = []
        for h in range(local):
            query = q_ref[pl.ds(t, Q_BLOCK), pl.ds(h * HD, HD)]
            turned = pltpu.roll(query, HD // 2, 1)
            rotated.append((query * cosine + turned * sine).astype(jnp.bfloat16))
        scores = lax.dot_general(
            jnp.concatenate(rotated, axis=0),
            k_ref[pl.ds(low, high - low), :],
            (((1,), (1,)), ((), ())),
            preferred_element_type=jnp.float32,
        ).reshape(local, *shape)
        scores = jnp.where(allowed[None], scores, -jnp.inf)
        top = jnp.max(scores, axis=2, keepdims=True)
        weights = jnp.exp2((scores - top) * turns)
        share = 1.0 / jnp.sum(weights, axis=2, keepdims=True)
        out = jnp.dot(
            (weights * share).astype(jnp.bfloat16).reshape(local * Q_BLOCK, high - low),
            v_ref[pl.ds(low, high - low), :],
            preferred_element_type=jnp.float32,
        ).astype(jnp.bfloat16)
        for h in range(local):
            att_ref[pl.ds(t, Q_BLOCK), pl.ds(h * HD, HD)] = out[h * Q_BLOCK : (h + 1) * Q_BLOCK]


def merge(me, b, mag, total, slots, w_list, w_at, x_list, x_at, sizes, xor, previous=None, attention=None):
    features, rows, tokens, rank = sizes
    width, count = b.shape[1], len(slots)
    first, last = previous is None, attention is not None
    plan = (slots, xor, rows, w_at, x_at, len(w_list), len(x_list), width // HD, first, last)
    vmem, hbm = pl.BlockSpec(memory_space=pltpu.VMEM), pl.BlockSpec(memory_space=pl.ANY)
    operands = [me, b, mag, total, *w_list, *x_list]
    in_specs = [pl.BlockSpec(memory_space=pltpu.SMEM)] + [vmem] * 3 + [hbm] * (len(w_list) + len(x_list))
    scratch = [
        pltpu.VMEM((count, rows, width), jnp.bfloat16),
        pltpu.VMEM((count, tokens, rows), jnp.bfloat16),
        pltpu.VMEM((count, rank, rows), jnp.bfloat16),
        pltpu.VMEM((count, rows, width), jnp.float32),
    ] + [pltpu.SemaphoreType.DMA((count,))] * 4
    if last:
        operands += list(attention)
        in_specs += [vmem] * 4 + [hbm] * 2
        scratch += [
            pltpu.VMEM((tokens, width), jnp.float32),
            pltpu.VMEM((tokens, HD), jnp.bfloat16),
            pltpu.VMEM((tokens, HD), jnp.bfloat16),
            pltpu.SemaphoreType.DMA((2,)),
        ]
    aliases = {}
    if not first:
        merged, query = previous
        operands += [query, merged]
        in_specs += [vmem, hbm]
        aliases = {len(operands) - 1: 0}
    return pl.pallas_call(
        functools.partial(merge_kernel, plan),
        out_shape=[
            jax.ShapeDtypeStruct((features, width), jnp.float32),
            jax.ShapeDtypeStruct((tokens, width), jnp.bfloat16 if last else jnp.float32),
        ],
        in_specs=in_specs,
        out_specs=[hbm, vmem],
        scratch_shapes=scratch,
        input_output_aliases=aliases,
        compiler_params=pltpu.CompilerParams(vmem_limit_bytes=48 * 1024 * 1024),
        cost_estimate=pl.CostEstimate(
            flops=2 * tokens * count * rows * width,
            bytes_accessed=count * rows * (6 * width + 2 * tokens),
            transcendentals=width // HD * tokens * tokens if last else 0,
        ),
    )(*operands)


def after(array, others):
    if not others:
        return array
    return lax.optimization_barrier((array, *others))[0]


ROUNDS = (
    ("z2", "z1", "y0", "s1", "w2", "s2", "s4"),
    ("z3", "y1", "y2", "w8", "w12"),
    ("y3", "cA", "w4", "w9", "w13"),
    ("cD", "s8", "w3", "w6", "w10", "w14"),
    ("w1", "w5", "w7", "w11", "w15"),
)
LINES = {"z1": ("x", 4), "z2": ("x", 8), "z3": ("z2", 4), "y0": ("x", 2), "y1": ("z1", 2), "y2": ("z2", 2), "y3": ("z3", 2)}
STACKS = {"cA": ("x", "z1", "z2", "y0"), "cD": ("z3", "y1", "y2", "y3")}
GROUPS = ((0, 8, 12, 4, 9, 2), (13, 10, 14, 6, 3), (5, 7, 1, 15), (11,))


def exchange(x, blocks, sums):
    def swap(array, d):
        return lax.ppermute(array, "tensor", [(i, i ^ d) for i in range(16)])

    got = {"x": x}
    partial = sums.reshape(8, 2, -1)

    def payload(name):
        if name in LINES:
            return got[LINES[name][0]], LINES[name][1]
        if name in STACKS:
            return jnp.stack([got[k] for k in STACKS[name]]), 1
        d = int(name[1:])
        return (partial[:, 1] if name[0] == "s" else blocks[d]), d

    def heavy(name):
        return name[0] in "ws"

    for k, names in enumerate(ROUNDS):
        new = {}
        for name in names:
            gates = [m for m in ROUNDS[k - 1] if not (heavy(name) and heavy(m))] if k else []
            gates += ROUNDS[k - 2] if k > 1 else ()
            array, d = payload(name)
            new[name] = swap(after(array, [got[m] for m in gates]), d)
            if name[0] == "s":
                partial = partial[:, 0] + new[name]
                if d < 8:
                    partial = partial.reshape(4 // d, 2, -1)
        got.update(new)
    x_list = [got[k] for k in ("x", "z1", "z2", "z3", "y0", "y1", "y2", "y3", "cA", "cD")]
    x_at = [None] * 16
    for k, d in enumerate((0, 4, 8, 12, 2, 6, 10, 14)):
        x_at[d] = (k, None)
    for k, d in enumerate((1, 5, 9, 3)):
        x_at[d] = (8, k)
    for k, d in enumerate((13, 7, 11, 15)):
        x_at[d] = (9, k)
    weights = [blocks[0]] + [got["w" + str(d)] for d in range(1, 16)]
    return x_list, x_at, weights, partial


def shards(
    check_hidden_input,
    query_base_matrix,
    adapter_input_factor,
    adapter_output_factor,
    magnitude,
    token_document_index,
    keys,
    values,
):
    n = lax.axis_size("tensor")
    my_index = lax.axis_index("tensor")
    rows, features = query_base_matrix.shape
    tokens, rank = check_hidden_input.shape[0], adapter_output_factor.shape[0]
    width = features // n
    me = my_index.astype(jnp.int32).reshape(1)
    b = lax.dynamic_slice_in_dim(adapter_output_factor, my_index * width, width, axis=1)
    mag = lax.dynamic_slice_in_dim(magnitude, my_index * width, width, axis=0)[None, :]
    cosine, sine = rope_tables(doc_positions(token_document_index))
    x = jnp.concatenate([check_hidden_input, adapter_input_factor.T], axis=0)
    attention = (cosine, sine, token_document_index[None, :], token_document_index[:, None], keys, values)
    sizes = (n * rows, rows, tokens, rank)
    if n == 16:
        blocks, sums = cut(me, adapter_input_factor, adapter_output_factor, query_base_matrix)
        x_list, x_at, weights, total = exchange(x, blocks, sums)
        done = None
        for k, slots in enumerate(GROUPS):
            used = sorted({x_at[d][0] for d in slots})
            done = merge(
                me, b, mag, total, slots,
                [weights[d] for d in slots], [(j, None) for j in range(len(slots))],
                [x_list[j] for j in used], [(used.index(x_at[d][0]), x_at[d][1]) for d in slots],
                sizes, True, done, attention if k == len(GROUPS) - 1 else None,
            )
        return done[0], done[1]
    x_all = lax.all_gather(x, "tensor", axis=0)
    w_cut = jnp.transpose(query_base_matrix.reshape(rows, n, width), (1, 0, 2))
    w_all = lax.all_to_all(w_cut, "tensor", split_axis=0, concat_axis=0, tiled=True)
    low_rank = lax.dot_general(x_all[:, tokens:], b, (((1,), (0,)), ((), ())), preferred_element_type=jnp.float32)
    total = jnp.sum(jnp.square(w_all.astype(jnp.float32) + low_rank), axis=(0, 1))[None, :]
    slots = tuple(range(n))
    at = [(0, d) for d in slots]
    merged, attended = merge(me, b, mag, total, slots, [w_all], at, [x_all], at, sizes, False, None, attention)
    return merged, attended


def solution(mesh):
    placed = (
        P("groups", "tensor"),
        P(("groups", "tensor"), None),
        P(("groups", "tensor"), None),
        P("groups", None),
        P("groups"),
        P("groups"),
        P("groups", None),
        P("groups", None),
    )
    return jax.shard_map(
        shards,
        mesh=mesh,
        in_specs=placed,
        out_specs=(P("groups", "tensor"), P("groups", "tensor")),
        check_vma=False,
    )
```

```python
import functools
import math

import jax
import jax.numpy as jnp
from jax import lax
from jax.experimental import pallas as pl
from jax.experimental.pallas import tpu as pltpu
from jax.sharding import PartitionSpec as P

HD = 128
KVH = 8
GROUP = 8
DOC_MAX = 512
Q_BLOCK = 128


def doc_positions(token_document_index):
    count = token_document_index.shape[0]
    index = jnp.arange(count, dtype=jnp.int32)
    starts = jnp.concatenate(
        [jnp.ones((1,), dtype=bool), token_document_index[1:] != token_document_index[:-1]]
    )
    first = lax.cummax(jnp.where(starts, index, jnp.int32(0)), axis=0)
    return (index - first).astype(jnp.float32)


def rope_tables(position):
    half = HD // 2
    freqs = 500000.0 ** (-(jnp.arange(half, dtype=jnp.float32) * 2.0 / HD))
    angle = position[:, None] * freqs[None, :]
    cosine = jnp.cos(angle)
    sine = jnp.sin(angle)
    return jnp.concatenate([cosine, cosine], axis=1), jnp.concatenate([-sine, sine], axis=1)


def cut_kernel(me_ref, a_ref, b_ref, w_ref, *refs):
    outs, sums_ref, (stage, in_sem, out_sem) = refs[:-4], refs[-4], refs[-3:]
    me = me_ref[0]
    n, _, width = stage.shape

    def column(e):
        return pl.multiple_of((me ^ e) * width, width)

    order = (8, 12, 9, 13, 4, 10, 14, 5, 11, 15, 6, 7, 2, 3, 1, 0)
    reads = {
        e: pltpu.make_async_copy(w_ref.at[:, pl.ds(column(e), width)], stage.at[e], in_sem.at[e])
        for e in order
    }
    writes = {e: pltpu.make_async_copy(stage.at[e], outs[e], out_sem.at[e]) for e in order}
    for e in order:
        reads[e].start()
    for e in order:
        reads[e].wait()
        writes[e].start()
        updated = stage[e].astype(jnp.float32) + jnp.dot(
            a_ref[...], b_ref[:, pl.ds(column(e), width)], preferred_element_type=jnp.float32
        )
        part = jnp.sum((updated * updated).reshape(-1, 8, width), axis=0)
        sums_ref[pl.ds(e, 1), :] = jnp.sum(part, axis=0, keepdims=True)
    for e in order:
        writes[e].wait()


def cut(me, a, b, w):
    rows, width = w.shape[0], w.shape[1] // 16
    vmem, hbm = pl.BlockSpec(memory_space=pltpu.VMEM), pl.BlockSpec(memory_space=pl.ANY)
    *blocks, sums = pl.pallas_call(
        cut_kernel,
        out_shape=[jax.ShapeDtypeStruct((rows, width), w.dtype)] * 16
        + [jax.ShapeDtypeStruct((16, width), jnp.float32)],
        in_specs=[pl.BlockSpec(memory_space=pltpu.SMEM), vmem, vmem, hbm],
        out_specs=[hbm] * 16 + [vmem],
        scratch_shapes=[
            pltpu.VMEM((16, rows, width), w.dtype),
            pltpu.SemaphoreType.DMA((16,)),
            pltpu.SemaphoreType.DMA((16,)),
        ],
        compiler_params=pltpu.CompilerParams(vmem_limit_bytes=24 * 1024 * 1024),
        cost_estimate=pl.CostEstimate(
            flops=4 * w.size, bytes_accessed=4 * w.size, transcendentals=0
        ),
    )(me, a, b, w)
    return blocks, sums


def merge_kernel(plan, me_ref, b_ref, mag_ref, total_ref, *refs):
    (slots, xor, rows, w_at, x_at, n_w, n_x, local, first, last) = plan
    w_refs, refs = refs[:n_w], refs[n_w:]
    x_refs, refs = refs[:n_x], refs[n_x:]
    if last:
        (cos_ref, sin_ref, row_ref, col_ref, k_ref, v_ref), refs = refs[:6], refs[6:]
    if not first:
        (q_in, _), refs = refs[:2], refs[2:]
    (merged_ref, q_out), refs = refs[:2], refs[2:]
    (w_buf, x_buf, a_buf, u_buf, w_sem, x_sem, a_sem, m_sem), refs = refs[:8], refs[8:]
    if last:
        q_buf, k_buf, v_buf, k_sem = refs
    else:
        q_buf = q_out
    tokens = x_buf.shape[1]
    me = me_ref[0]
    count = len(slots)

    def part(refs, spot):
        which, index = spot
        return refs[which] if index is None else refs[which].at[index]

    def w_copy(k):
        return pltpu.make_async_copy(part(w_refs, w_at[k]), w_buf.at[k], w_sem.at[k])

    def x_copy(k):
        src = part(x_refs, x_at[k]).at[pl.ds(0, tokens)]
        return pltpu.make_async_copy(src, x_buf.at[k], x_sem.at[k])

    def a_copy(k):
        src = part(x_refs, x_at[k]).at[pl.ds(tokens, a_buf.shape[1])]
        return pltpu.make_async_copy(src, a_buf.at[k], a_sem.at[k])

    def out_copy(k):
        row = pl.multiple_of(((me ^ slots[k]) if xor else slots[k]) * rows, rows)
        return pltpu.make_async_copy(u_buf.at[k], merged_ref.at[pl.ds(row, rows), :], m_sem.at[k])

    for k in range(count):
        w_copy(k).start()
        a_copy(k).start()
        x_copy(k).start()
    if last:
        column = pl.multiple_of(me * local // GROUP * HD, HD)
        kv_copies = [
            pltpu.make_async_copy(ref.at[:, pl.ds(column, HD)], buf, k_sem.at[j])
            for j, (ref, buf) in enumerate(((k_ref, k_buf), (v_ref, v_buf)))
        ]
        for copy in kv_copies:
            copy.start()

    scale = mag_ref[...] / jnp.sqrt(total_ref[...] + 1e-06)
    for k in range(count):
        w_copy(k).wait()
        a_copy(k).wait()
        updated = w_buf[k].astype(jnp.float32) + lax.dot_general(
            a_buf[k], b_ref[...], (((0,), (0,)), ((), ())), preferred_element_type=jnp.float32
        )
        merged = updated * scale
        u_buf[k] = merged
        out_copy(k).start()
        x_copy(k).wait()
        product = jnp.dot(x_buf[k], merged.astype(jnp.bfloat16), preferred_element_type=jnp.float32)
        if k > 0:
            q_buf[...] += product
        elif first:
            q_buf[...] = product
        else:
            q_buf[...] = q_in[...] + product

    if last:
        for copy in kv_copies:
            copy.wait()
        attend(q_buf, cos_ref, sin_ref, row_ref, col_ref, k_buf, v_buf, q_out, local)
    for k in range(count):
        out_copy(k).wait()


def attend(q_ref, cos_ref, sin_ref, row_ref, col_ref, k_ref, v_ref, att_ref, local):
    tokens = q_ref.shape[0]
    turns = jnp.float32(HD**-0.5 * math.log2(math.e))
    for t in range(0, tokens, Q_BLOCK):
        low, high = max(0, t - DOC_MAX), t + Q_BLOCK
        shape = (Q_BLOCK, high - low)
        later = lax.broadcasted_iota(jnp.int32, shape, 0) + (t - low)
        allowed = (lax.broadcasted_iota(jnp.int32, shape, 1) <= later) & (
            row_ref[:, pl.ds(low, high - low)] == col_ref[pl.ds(t, Q_BLOCK), :]
        )
        cosine, sine = cos_ref[pl.ds(t, Q_BLOCK), :], sin_ref[pl.ds(t, Q_BLOCK), :]
        rotated = []
        for h in range(local):
            query = q_ref[pl.ds(t, Q_BLOCK), pl.ds(h * HD, HD)]
            turned = pltpu.roll(query, HD // 2, 1)
            rotated.append((query * cosine + turned * sine).astype(jnp.bfloat16))
        scores = lax.dot_general(
            jnp.concatenate(rotated, axis=0),
            k_ref[pl.ds(low, high - low), :],
            (((1,), (1,)), ((), ())),
            preferred_element_type=jnp.float32,
        ).reshape(local, *shape)
        scores = jnp.where(allowed[None], scores, -jnp.inf)
        top = jnp.max(scores, axis=2, keepdims=True)
        weights = jnp.exp2((scores - top) * turns)
        share = 1.0 / jnp.sum(weights, axis=2, keepdims=True)
        out = jnp.dot(
            (weights * share).astype(jnp.bfloat16).reshape(local * Q_BLOCK, high - low),
            v_ref[pl.ds(low, high - low), :],
            preferred_element_type=jnp.float32,
        ).astype(jnp.bfloat16)
        for h in range(local):
            att_ref[pl.ds(t, Q_BLOCK), pl.ds(h * HD, HD)] = out[h * Q_BLOCK : (h + 1) * Q_BLOCK]


def merge(me, b, mag, total, slots, w_list, w_at, x_list, x_at, sizes, xor, previous=None, attention=None):
    features, rows, tokens, rank = sizes
    width, count = b.shape[1], len(slots)
    first, last = previous is None, attention is not None
    plan = (slots, xor, rows, w_at, x_at, len(w_list), len(x_list), width // HD, first, last)
    vmem, hbm = pl.BlockSpec(memory_space=pltpu.VMEM), pl.BlockSpec(memory_space=pl.ANY)
    operands = [me, b, mag, total, *w_list, *x_list]
    in_specs = [pl.BlockSpec(memory_space=pltpu.SMEM)] + [vmem] * 3 + [hbm] * (len(w_list) + len(x_list))
    scratch = [
        pltpu.VMEM((count, rows, width), jnp.bfloat16),
        pltpu.VMEM((count, tokens, rows), jnp.bfloat16),
        pltpu.VMEM((count, rank, rows), jnp.bfloat16),
        pltpu.VMEM((count, rows, width), jnp.float32),
    ] + [pltpu.SemaphoreType.DMA((count,))] * 4
    if last:
        operands += list(attention)
        in_specs += [vmem] * 4 + [hbm] * 2
        scratch += [
            pltpu.VMEM((tokens, width), jnp.float32),
            pltpu.VMEM((tokens, HD), jnp.bfloat16),
            pltpu.VMEM((tokens, HD), jnp.bfloat16),
            pltpu.SemaphoreType.DMA((2,)),
        ]
    aliases = {}
    if not first:
        merged, query = previous
        operands += [query, merged]
        in_specs += [vmem, hbm]
        aliases = {len(operands) - 1: 0}
    return pl.pallas_call(
        functools.partial(merge_kernel, plan),
        out_shape=[
            jax.ShapeDtypeStruct((features, width), jnp.float32),
            jax.ShapeDtypeStruct((tokens, width), jnp.bfloat16 if last else jnp.float32),
        ],
        in_specs=in_specs,
        out_specs=[hbm, vmem],
        scratch_shapes=scratch,
        input_output_aliases=aliases,
        compiler_params=pltpu.CompilerParams(vmem_limit_bytes=48 * 1024 * 1024),
        cost_estimate=pl.CostEstimate(
            flops=2 * tokens * count * rows * width,
            bytes_accessed=count * rows * (6 * width + 2 * tokens),
            transcendentals=width // HD * tokens * tokens if last else 0,
        ),
    )(*operands)


def after(array, others):
    if not others:
        return array
    return lax.optimization_barrier((array, *others))[0]


ROUNDS = (
    ("z2", "z1", "y0", "s1", "w2", "s2", "s4"),
    ("z3", "y1", "y2", "w8", "w12"),
    ("y3", "cA", "w4", "w10", "w14"),
    ("cD", "s8", "w3", "w6", "w9", "w13"),
    ("w1", "w5", "w7", "w11", "w15"),
)
LINES = {"z1": ("x", 4), "z2": ("x", 8), "z3": ("z2", 4), "y0": ("x", 2), "y1": ("z1", 2), "y2": ("z2", 2), "y3": ("z3", 2)}
STACKS = {"cA": ("x", "z1", "z2", "y0"), "cD": ("z3", "y1", "y2", "y3")}
GROUPS = ((0, 8, 12, 4, 10, 2), (13, 9, 14, 6, 3), (5, 7, 1, 15), (11,))


def exchange(x, blocks, sums):
    def swap(array, d):
        return lax.ppermute(array, "tensor", [(i, i ^ d) for i in range(16)])

    got = {"x": x}
    partial = sums.reshape(8, 2, -1)

    def payload(name):
        if name in LINES:
            return got[LINES[name][0]], LINES[name][1]
        if name in STACKS:
            return jnp.stack([got[k] for k in STACKS[name]]), 1
        d = int(name[1:])
        return (partial[:, 1] if name[0] == "s" else blocks[d]), d

    def heavy(name):
        return name[0] in "ws"

    for k, names in enumerate(ROUNDS):
        new = {}
        for name in names:
            gates = [m for m in ROUNDS[k - 1] if not (heavy(name) and heavy(m))] if k else []
            gates += ROUNDS[k - 2] if k > 1 else ()
            array, d = payload(name)
            new[name] = swap(after(array, [got[m] for m in gates]), d)
            if name[0] == "s":
                partial = partial[:, 0] + new[name]
                if d < 8:
                    partial = partial.reshape(4 // d, 2, -1)
        got.update(new)
    x_list = [got[k] for k in ("x", "z1", "z2", "z3", "y0", "y1", "y2", "y3", "cA", "cD")]
    x_at = [None] * 16
    for k, d in enumerate((0, 4, 8, 12, 2, 6, 10, 14)):
        x_at[d] = (k, None)
    for k, d in enumerate((1, 5, 9, 3)):
        x_at[d] = (8, k)
    for k, d in enumerate((13, 7, 11, 15)):
        x_at[d] = (9, k)
    weights = [blocks[0]] + [got["w" + str(d)] for d in range(1, 16)]
    return x_list, x_at, weights, partial


def shards(
    check_hidden_input,
    query_base_matrix,
    adapter_input_factor,
    adapter_output_factor,
    magnitude,
    token_document_index,
    keys,
    values,
):
    n = lax.axis_size("tensor")
    my_index = lax.axis_index("tensor")
    rows, features = query_base_matrix.shape
    tokens, rank = check_hidden_input.shape[0], adapter_output_factor.shape[0]
    width = features // n
    me = my_index.astype(jnp.int32).reshape(1)
    b = lax.dynamic_slice_in_dim(adapter_output_factor, my_index * width, width, axis=1)
    mag = lax.dynamic_slice_in_dim(magnitude, my_index * width, width, axis=0)[None, :]
    cosine, sine = rope_tables(doc_positions(token_document_index))
    x = jnp.concatenate([check_hidden_input, adapter_input_factor.T], axis=0)
    attention = (cosine, sine, token_document_index[None, :], token_document_index[:, None], keys, values)
    sizes = (n * rows, rows, tokens, rank)
    if n == 16:
        blocks, sums = cut(me, adapter_input_factor, adapter_output_factor, query_base_matrix)
        x_list, x_at, weights, total = exchange(x, blocks, sums)
        done = None
        for k, slots in enumerate(GROUPS):
            used = sorted({x_at[d][0] for d in slots})
            done = merge(
                me, b, mag, total, slots,
                [weights[d] for d in slots], [(j, None) for j in range(len(slots))],
                [x_list[j] for j in used], [(used.index(x_at[d][0]), x_at[d][1]) for d in slots],
                sizes, True, done, attention if k == len(GROUPS) - 1 else None,
            )
        return done[0], done[1]
    x_all = lax.all_gather(x, "tensor", axis=0)
    w_cut = jnp.transpose(query_base_matrix.reshape(rows, n, width), (1, 0, 2))
    w_all = lax.all_to_all(w_cut, "tensor", split_axis=0, concat_axis=0, tiled=True)
    low_rank = lax.dot_general(x_all[:, tokens:], b, (((1,), (0,)), ((), ())), preferred_element_type=jnp.float32)
    total = jnp.sum(jnp.square(w_all.astype(jnp.float32) + low_rank), axis=(0, 1))[None, :]
    slots = tuple(range(n))
    at = [(0, d) for d in slots]
    merged, attended = merge(me, b, mag, total, slots, [w_all], at, [x_all], at, sizes, False, None, attention)
    return merged, attended


def solution(mesh):
    placed = (
        P("groups", "tensor"),
        P(("groups", "tensor"), None),
        P(("groups", "tensor"), None),
        P("groups", None),
        P("groups"),
        P("groups"),
        P("groups", None),
        P("groups", None),
    )
    return jax.shard_map(
        shards,
        mesh=mesh,
        in_specs=placed,
        out_specs=(P("groups", "tensor"), P("groups", "tensor")),
        check_vma=False,
    )
```
